1024 devices in a mesh: expert: 64 (over z, core), seq: 16 (over y, x).
Axes of the slice: x: 4, y: 4, z: 32, core: 2. Of those that a mesh axis runs over, the one named last changes fastest.
Arguments:
- tokens: bfloat16 [8192, 4096], P('expert', 'seq'), may hold values from -6 to 6
- out_grad: bfloat16 [8192, 4096], P('expert', 'seq'), may hold values from -6 to 6
- expert_ids: int32 [8192, 8], P('expert'), may hold values from 0 to 63, all different within a row; in each aligned block of 128 rows (0 to 127, 128 to 255, ...) at most 20 rows name the same one
- router_probs: float32 [8192, 8], P('expert'), may hold values from 0.05 to 0.5
- keep_mask: int32 [8192, 8], P('expert'), may hold values 0 or 1
- gate_saved: bfloat16 [64, 1280, 768], P('expert', 'seq'), may hold values from -6 to 6
- up_saved: bfloat16 [64, 1280, 768], P('expert', 'seq'), may hold values from -6 to 6
- w_gate: bfloat16 [64, 4096, 768], P('expert', 'seq'), may hold values from -0.09375 to 0.09375
- w_up: bfloat16 [64, 4096, 768], P('expert', 'seq'), may hold values from -0.09375 to 0.09375
- w_down: bfloat16 [64, 768, 4096], P('expert', None, 'seq'), may hold values from -0.21875 to 0.21875
Outputs:
- input_grad: bfloat16 [8192, 4096], P('expert', 'seq')
- gate_wgrad: bfloat16 [64, 4096, 768], P('expert', 'seq')
- up_wgrad: bfloat16 [64, 4096, 768], P('expert', 'seq')
- down_wgrad: bfloat16 [64, 768, 4096], P('expert', None, 'seq')
The draws below stay inside these ranges and needn't reach their ends.
Inputs may be any that keep to these rules, and one draw needn't show every extreme that they name: `expert_ids`: each row names 8 different experts; within the 128 rows of one block no expert is named by more than 20 rows, a bound that some block reaches.
All inputs are finite; a program needn't handle non-finite values. No bound on the sum of `keep_mask` on one device may be relied on, other than what follows from the above.
Results may differ from the reference program's by a relative error of at most 0.023.
Values may be sent and summed in bfloat16 or wider, within the bound.
A program may use at most 32 MiB of HBM per device.

```python
import math
import jax
import jax.numpy as jnp
import numpy as np
from jax import lax

D = 4096
FF = 768
TOPK = 8
TOK_DEV = 128
EXPERTS = 64
CAP = 20
SLOTS = 1280
TOKENS = 8192
N_EXPERT = 64
N_SEQ = 16


def plant(drawn, own_key, low, largest):
    longest = drawn.shape.index(max(drawn.shape))
    spots = []
    for shift in (0, 1):
        where = [jax.random.randint(jax.random.fold_in(own_key, axis), (), 0, length) for axis, length in enumerate(drawn.shape)]
        where[longest] = (where[longest] + shift) % drawn.shape[longest]
        spots.append(tuple(where))
    return drawn.at[spots[0]].set(low).at[spots[1]].set(largest)


def shard_levels(stream_key, dims, cuts, low, top_value):
    factor_of, own = 1.0, jax.random.fold_in(stream_key, 6)
    for axis_at, parts in cuts:
        heights = jnp.exp(jax.random.uniform(jax.random.fold_in(own, axis_at), (parts,), jnp.float32, low / len(cuts), top_value / len(cuts)))
        factor_of = factor_of * jnp.repeat(heights, dims[axis_at] // parts).reshape([-1 if axis == axis_at else 1 for axis in range(len(dims))])
    return factor_of


def shared_out(stream_key, own, number, rows, amount, top, most, skew):
    ranking = jax.random.permutation(stream_key, amount)
    heavy_load, ordinary = shares(amount, rows * top, most, skew, True), shares(amount, rows * top, most, skew, False)
    places = jnp.arange(amount)

    def named(lengths, turn):
        used = int((lengths > 0).sum())
        fixed = max(1, used // 4)
        passed = fixed + (places - fixed + turn * (used - fixed)) % max(1, amount - fixed)
        return jnp.zeros((amount,), jnp.int32).at[ranking[jnp.where(places < fixed, places, passed)]].set(jnp.asarray(lengths, jnp.int32))

    lengths = jnp.where(number % 4 == 0, named(heavy_load, number // 4), named(ordinary, number - number // 4 - 1))
    mixed = jax.random.permutation(jax.random.fold_in(own, 3), amount)
    source_of, sink = mixed[0:amount // 2 * 2:2], mixed[1:amount // 2 * 2:2]
    margin = jnp.minimum(lengths[source_of] - 1, most - lengths[sink]) // 2
    margin = jnp.where((source_of == ranking[0]) | (sink == ranking[0]) | (lengths[sink] == 0), 0, jnp.maximum(margin, 0))
    passed = jax.random.randint(jax.random.fold_in(own, 4), (amount // 2,), 0, 1 << 20) % (margin + 1)
    lengths = lengths.at[source_of].add(-passed).at[sink].add(passed)
    items = jnp.searchsorted(jnp.cumsum(lengths), jnp.arange(rows * top), side="right").astype(jnp.int32)
    listing = items.reshape(top, rows).T
    listing = listing[jax.random.permutation(jax.random.fold_in(own, 1), rows)]
    turn = jax.random.randint(jax.random.fold_in(own, 2), (rows, 1), 0, top)
    return jnp.take_along_axis(listing, (jnp.arange(top)[None, :] + turn) % top, axis=1)


def shares(amount, total, most, slope, full):
    loads = [(1 << 20) // math.isqrt(grade ** slope) + 1 for grade in range(1, amount + 1)]
    largest = most if full else min(most, max(-(-total // amount), total * loads[0] // sum(loads)))
    least = 1 if total - largest >= amount - 1 else 0
    given, rest = [largest] + [least] * (amount - 1), total - largest - least * (amount - 1)
    while rest > 0:
        free = [i for i in range(1, amount) if given[i] < largest] or [i for i in range(1, amount) if given[i] < most]
        pool, budget = sum([loads[i] for i in free]), rest
        for i in free:
            extra = min(most - given[i], max(1, budget * loads[i] // pool), rest)
            given[i] = given[i] + extra
            rest = rest - extra
    return np.array(given)


def normal_values(rng, extent, width, most, split=(), held_as=jnp.bfloat16):
    array = jax.random.normal(rng, extent, jnp.float32) * width
    if len(split) > 0:
        array = shard_levels(rng, extent, split, -0.22, 0.18) * array
    return jnp.clip(array, min=-most, max=most).astype(held_as)


def setup_inputs(seed: int = 0) -> dict:
    seeds = jax.random.split(jax.random.key(seed), 11)
    tokens = normal_values(seeds[0], (TOKENS, D), 1.0, 6.0, ((0, 64), (1, 16)))
    out_grad = normal_values(seeds[1], (TOKENS, D), 1.0, 6.0, ((0, 64), (1, 16)))
    expert_ids_keys = jax.random.split(jax.random.fold_in(seeds[2], 1), TOKENS // TOK_DEV)
    expert_ids_turns = jax.random.permutation(jax.random.fold_in(seeds[2], 3), TOKENS // TOK_DEV)
    expert_ids = jax.vmap(lambda own, number: shared_out(jax.random.fold_in(seeds[2], 2), own, number, TOK_DEV, EXPERTS, TOPK, CAP, 2))(expert_ids_keys, expert_ids_turns).reshape((TOKENS, TOPK))
    router_probs = jnp.clip(jnp.exp(math.log(0.5) - 2.3025851 * jax.random.uniform(seeds[3], (TOKENS, TOPK), jnp.float32) ** shard_levels(seeds[3], (TOKENS, TOPK), ((0, 64),), -0.2, 0.2)), 0.05, 0.5)
    keep_mask = plant((jax.random.randint(seeds[4], (TOKENS, TOPK), 0, 8) < 7).astype(jnp.int32), jax.random.fold_in(seeds[4], 1), 0, 1)
    gate_saved = normal_values(seeds[5], (EXPERTS, SLOTS, FF), 1.0, 6.0, ((0, 64), (1, 16)))
    up_saved = normal_values(seeds[6], (EXPERTS, SLOTS, FF), 1.0, 6.0, ((0, 64), (1, 16)))
    w_gate = normal_values(seeds[7], (EXPERTS, D, FF), D ** -0.5, 0.09375, ((0, 64), (1, 16)))
    w_up = normal_values(seeds[8], (EXPERTS, D, FF), D ** -0.5, 0.09375, ((0, 64), (1, 16)))
    w_down = normal_values(seeds[9], (EXPERTS, FF, D), FF ** -0.5, 0.21875, ((0, 64), (2, 16)))
    return {"tokens": tokens, "out_grad": out_grad, "expert_ids": expert_ids, "router_probs": router_probs, "keep_mask": keep_mask, "gate_saved": gate_saved, "up_saved": up_saved, "w_gate": w_gate, "w_up": w_up, "w_down": w_down}


def swiglu_backward(hidden_grad, gate_in, up_in):
    gate_f = gate_in.astype(jnp.float32)
    up_f = up_in.astype(jnp.float32)
    sigmoid_g = jax.nn.sigmoid(gate_f)
    silu_g = gate_f * sigmoid_g
    hidden = (silu_g * up_f).astype(jnp.bfloat16)
    gate_grad = (hidden_grad * up_f * sigmoid_g * (1.0 + gate_f * (1.0 - sigmoid_g))).astype(jnp.bfloat16)
    up_grad = (hidden_grad * silu_g).astype(jnp.bfloat16)
    return hidden, gate_grad, up_grad


def one_expert(operands):
    expert_in, expert_grad, gate_in, up_in, gate_w, up_w, down_w = operands
    width_part = D // N_SEQ
    grad_groups = expert_grad.reshape(SLOTS, N_SEQ, width_part).astype(jnp.float32)
    down_groups = down_w.reshape(FF, N_SEQ, width_part).astype(jnp.float32)
    partial_value = jnp.einsum("rsd,fsd->srf", grad_groups, down_groups)
    rounded = lax.optimization_barrier(partial_value.astype(jnp.bfloat16))
    hidden_grad = jnp.sum(rounded.astype(jnp.float32), axis=0)
    hidden, gate_grad, up_grad = swiglu_backward(hidden_grad, gate_in, up_in)
    down_grad = jnp.dot(hidden.T, expert_grad, preferred_element_type=jnp.float32).astype(jnp.bfloat16)
    gate_wgrad = jnp.dot(expert_in.T, gate_grad, preferred_element_type=jnp.float32).astype(jnp.bfloat16)
    up_wgrad = jnp.dot(expert_in.T, up_grad, preferred_element_type=jnp.float32).astype(jnp.bfloat16)
    slot_back = (jnp.dot(gate_grad, gate_w.T, preferred_element_type=jnp.float32)
                 + jnp.dot(up_grad, up_w.T, preferred_element_type=jnp.float32)).astype(jnp.bfloat16)
    return slot_back, gate_wgrad, up_wgrad, down_grad


def reference(tokens, out_grad, expert_ids, router_probs, keep_mask, gate_saved, up_saved, w_gate, w_up, w_down):
    routed = expert_ids.reshape(N_EXPERT, TOK_DEV * TOPK)
    onehot = (routed[:, :, None] == jnp.arange(EXPERTS, dtype=jnp.int32)[None, None, :]).astype(jnp.int32)
    before = jnp.cumsum(onehot, axis=1) - onehot
    position = jnp.sum(before * onehot, axis=2).astype(jnp.int32)
    source = jnp.arange(N_EXPERT, dtype=jnp.int32)[:, None]
    slot_row = source * CAP + position
    flat_slot = (routed * SLOTS + slot_row).reshape(-1).astype(jnp.int32)
    repeated = jnp.repeat(tokens, TOPK, axis=0)
    weights = (router_probs * keep_mask.astype(jnp.float32)).reshape(-1, 1)
    scaled = (weights * jnp.repeat(out_grad.astype(jnp.float32), TOPK, axis=0)).astype(jnp.bfloat16)
    expert_in = jnp.zeros((EXPERTS * SLOTS, D), jnp.bfloat16).at[flat_slot].set(repeated).reshape(EXPERTS, SLOTS, D)
    expert_grad = jnp.zeros((EXPERTS * SLOTS, D), jnp.bfloat16).at[flat_slot].set(scaled).reshape(EXPERTS, SLOTS, D)
    slot_back, gate_wgrad, up_wgrad, down_wgrad = lax.map(
        one_expert, (expert_in, expert_grad, gate_saved, up_saved, w_gate, w_up, w_down))
    picked = slot_back.reshape(EXPERTS * SLOTS, D)[flat_slot]
    input_grad = jnp.sum(picked.reshape(TOKENS, TOPK, D).astype(jnp.float32), axis=1).astype(jnp.bfloat16)
    return input_grad, gate_wgrad, up_wgrad, down_wgrad
```

```python
import functools

import jax
import jax.numpy as jnp
from jax import lax
from jax.experimental import pallas as pl
from jax.experimental.pallas import tpu as pltpu
from jax.sharding import PartitionSpec as P

MESH = pl.DeviceIdType.MESH
F32 = jnp.float32
BF16 = jnp.bfloat16


def dot_nt(a, b):
    return lax.dot_general(a, b, (((1,), (1,)), ((), ())), preferred_element_type=F32)


def dot_tn(a, b):
    return lax.dot_general(a, b, (((0,), (0,)), ((), ())), preferred_element_type=F32)


def dot_nn(a, b):
    return lax.dot_general(a, b, (((1,), (0,)), ((), ())), preferred_element_type=F32)


def layer_kernel(
    nz, side, cap,
    tok_ref, og_ref, ids_ref, prob_ref, keep_ref, gate_ref, up_ref, wg_ref, wu_ref, wd_ref,
    ig_ref, gw_ref, uw_ref, dw_ref,
    og_all, tok_all, gu_all, pbuf, rsbuf, hg_all, gg, ug, hid, gs, xs, sb, sbs, pos_ref, contrib, rbuf,
    og_s, og_r, og_ss, og_sr, tk_s, tk_r, tk_ss, tk_sr, gu_s, gu_r, rs_s, rs_r, ag_s, ag_r, sb_s, sb_r,
    cb_s, cb_r,
):
    ns = side * side
    ec = lax.axis_index("expert")
    s = lax.axis_index("seq")
    z, c = ec >> 1, ec & 1
    sy, sx = s // side, s % side
    half_ring = nz // 2
    reach = half_ring // 2
    far = reach + 1
    limit = (half_ring, half_ring - 1)
    n_chunks = nz // 2
    quarter = reach // 2
    tok_rows = og_ref.shape[0]
    rows = 4 * cap
    hw = gate_ref.shape[1] // 2
    per_group = n_chunks // 2

    def at_z(k):
        return (z + k) & (nz - 1)

    def dev(e, q):
        return {"expert": e, "seq": q}

    def remote(src, dst, ssem, rsem, device):
        return pltpu.make_async_remote_copy(
            src, dst, ssem, rsem, device_id=device, device_id_type=MESH
        )

    bar = pltpu.get_barrier_semaphore()
    hops = sorted({1, nz - 1, far, nz - far})
    for k in hops:
        pl.semaphore_signal(bar, inc=1, device_id=dev(at_z(k) * 2 + c, s), device_id_type=MESH)
    pl.semaphore_signal(bar, inc=1, device_id=dev(ec ^ 1, s), device_id_type=MESH)

    def greet(k, carry):
        pl.semaphore_signal(bar, inc=1, device_id=dev(ec, (s + k) & (ns - 1)), device_id_type=MESH)
        return carry

    lax.fori_loop(1, ns, greet, 0)

    weight = prob_ref[...] * keep_ref[...].astype(F32)
    w_hi = weight.astype(BF16).astype(F32)
    w_mid = (weight - w_hi).astype(BF16).astype(F32)
    w_lo = (weight - w_hi) - w_mid
    top = jnp.concatenate([ids_ref[...].astype(F32), w_mid], axis=1)
    low = jnp.concatenate([w_hi, w_lo], axis=1)
    og_all[ec, pl.ds(0, tok_rows), :] = og_ref[...]
    og_all[ec, pl.ds(tok_rows, 16), :] = jnp.concatenate([top, low], axis=0).astype(BF16)
    tok_all[ec] = tok_ref[...]
    for h in range(2):
        gu_all[s, h, 0] = gate_ref[:, h * hw : (h + 1) * hw]
        gu_all[s, h, 1] = up_ref[:, h * hw : (h + 1) * hw]
    pl.semaphore_wait(bar, len(hops) + 1 + ns - 1)

    def zslot(way, d, core):
        return at_z(nz - d if way == 0 else d) * 2 + core

    def ring_send(buf, ssem, rsem, way, d, child):
        k = child - d
        slot = zslot(way, d, c)
        target = at_z(k if way == 0 else nz - k) * 2 + c
        return remote(
            buf.at[slot], buf.at[slot], ssem.at[way, child], rsem.at[way, child], dev(target, s)
        )

    def ring_landed(buf, ssem, rsem, way, d):
        slot = buf.at[zslot(way, d, c)]
        remote(slot, slot, ssem.at[way, d], rsem.at[way, d], dev(ec, s)).wait_recv()

    def sib_copy(buf, ssem, rsem, way, d, core):
        slot = buf.at[zslot(way, d, core)]
        return remote(slot, slot, ssem.at[way, d], rsem.at[way, d], dev(ec ^ 1, s))

    og_x = (og_all, og_s, og_r)
    og_sib = (og_all, og_ss, og_sr)
    tk_x = (tok_all, tk_s, tk_r)
    tk_sib = (tok_all, tk_ss, tk_sr)

    for way in (0, 1):
        ring_send(*og_x, way, 0, 1).start()
        ring_send(*og_x, way, 0, far).start()
    sib_copy(*og_sib, 0, 0, c).start()

    def seq_of(y, x):
        return (y & (side - 1)) * side + (x & (side - 1))

    def gu_peer(h, phase, k):
        return seq_of(sy, sx + k) if (h == phase) else seq_of(sy + k, sx)

    def gu_slot(h, j):
        return seq_of(sy, sx + j) if h == 0 else seq_of(sy + j, sx)

    def gu_first(h, k):
        return remote(
            gu_all.at[s, h], gu_all.at[s, h], gu_s.at[h, 0, k], gu_r.at[h, 0, k],
            dev(ec, gu_peer(h, 0, k)),
        )

    def gu_second(h, j, k):
        slot = gu_all.at[gu_slot(h, j), h]
        return remote(
            slot, slot, gu_s.at[h, 1 + j, k], gu_r.at[h, 1 + j, k], dev(ec, gu_peer(h, 1, k))
        )

    def gu_landed(slot, h, a, k):
        ref = gu_all.at[slot, h]
        remote(ref, ref, gu_s.at[h, a, k], gu_r.at[h, a, k], dev(ec, s)).wait_recv()

    for k in range(1, side):
        for h in range(2):
            gu_first(h, k).start()
    for k in range(1, side):
        for h in range(2):
            gu_second(h, 0, k).start()
    for way in (0, 1):
        ring_send(*tk_x, way, 0, 1).start()
    sib_copy(*tk_sib, 0, 0, c).start()

    def og_step(k):
        for way in (0, 1):
            ring_landed(*og_x, way, k)

            @pl.when(k < reach)
            def _():
                ring_send(*og_x, way, k, k + 1).start()

            sib_copy(*og_sib, way, k, c).start()

            def far_part():
                ring_landed(*og_x, way, reach + k)

                @pl.when(reach + k < limit[way])
                def _():
                    ring_send(*og_x, way, reach + k, reach + k + 1).start()

                sib_copy(*og_sib, way, reach + k, c).start()

            if way == 0:
                far_part()
            else:
                pl.when(reach + k <= limit[1])(far_part)

    def og_sib_wait(k):
        for way in (0, 1):
            sib_copy(*og_sib, way, k, 1 - c).wait_recv()
            if way == 0:
                sib_copy(*og_sib, way, reach + k, 1 - c).wait_recv()
            else:

                @pl.when(reach + k <= limit[1])
                def _():
                    sib_copy(*og_sib, way, reach + k, 1 - c).wait_recv()

    def tok_step(d, carry):
        for way in (0, 1):

            def part():
                ring_landed(*tk_x, way, d)

                @pl.when(d < limit[way])
                def _():
                    ring_send(*tk_x, way, d, d + 1).start()

                sib_copy(*tk_sib, way, d, c).start()

            if way == 0:
                part()
            else:
                pl.when(d <= limit[1])(part)
        return carry

    row80 = lax.broadcasted_iota(jnp.int32, (rows, tok_rows), 0).astype(F32)
    row8 = lax.broadcasted_iota(jnp.int32, (8, tok_rows), 0)
    before = (
        lax.broadcasted_iota(jnp.int32, (tok_rows, tok_rows), 0)
        < lax.broadcasted_iota(jnp.int32, (tok_rows, tok_rows), 1)
    ).astype(F32).astype(BF16)

    def chunk_at(offset):
        return ((z >> 1) + offset) & (n_chunks - 1)

    def chunk_of(o):
        m = ((o - 1) >> 2) + 1
        r = (o - 1) & 3
        last = o - (n_chunks - 3)
        plain = (m + jnp.where(r >= 2, quarter, 0)) * jnp.where((r & 1) == 1, -1, 1)
        tail = jnp.where(last == 0, quarter, jnp.where(last == 1, -quarter, n_chunks // 2))
        off = jnp.where(o == 0, 0, jnp.where(last >= 0, tail, plain))
        return chunk_at(off + n_chunks)

    def pick(o, carry):
        i = chunk_of(o)
        member = jnp.zeros((8, tok_rows), F32)
        ws = []
        for q in range(4):
            meta = og_all[4 * i + q, pl.ds(tok_rows, 16), :].astype(F32)
            ids = meta[0:8, 0:tok_rows]
            w = (meta[8:16, 0:tok_rows] + meta[0:8, tok_rows:]) + meta[8:16, tok_rows:]
            for t in range(2):
                own = (ids == (ec if t == 0 else ec ^ 1).astype(F32)).astype(F32)
                member = jnp.where(
                    row8 == t * 4 + q, jnp.sum(own, axis=0, keepdims=True), member
                )
                if t == 0:
                    ws.append(jnp.sum(own * w, axis=0, keepdims=True))
        count = dot_nn(member.astype(BF16), before)
        place = jnp.where(member > 0.5, count + ((row8 & 3) * cap).astype(F32), -1000.0)
        pos_ref[i] = place
        total = jnp.zeros((rows, og_ref.shape[1]), F32)
        wsum = jnp.zeros((rows, 1), F32)
        for q in range(4):
            hot = (row80 == place[q : q + 1, :]).astype(F32)
            total += dot_nn(hot.astype(BF16), og_all[4 * i + q, pl.ds(0, tok_rows), :])
            wsum += jnp.sum(hot * ws[q], axis=1, keepdims=True)
        gs[o] = (total * wsum).astype(BF16)
        return carry

    def partial_products(m, count):
        left = gs[pl.ds(m, count)].reshape(count * rows, gs.shape[2])
        out = dot_nt(left, wd_ref[...]).astype(BF16)
        for r in range(count):
            o = m + r
            for h in range(2):
                pbuf[o * 2 + h] = out[r * rows : (r + 1) * rows, h * hw : (h + 1) * hw]

    def rs_copy(g, k):
        j = (s + k) & (ns - 1)
        return remote(
            pbuf.at[g * ns + j], rsbuf.at[g, s], rs_s.at[g, k], rs_r.at[g, k], dev(ec, j)
        )

    def rs_start(g):
        def go(k, carry):
            rs_copy(g, k).start()
            return carry

        lax.fori_loop(1, ns, go, 0)
        rsbuf[g, s] = pbuf[g * ns + s]

    def ag_copy(g, k):
        piece = hg_all.at[g * ns + s]
        return remote(piece, piece, ag_s.at[g, k], ag_r.at[g, k], dev(ec, (s + k) & (ns - 1)))

    def rs_finish(g):
        def landed(k, carry):
            slot = rsbuf.at[g, (s - k) & (ns - 1)]
            remote(slot, slot, rs_s.at[g, k], rs_r.at[g, k], dev(ec, s)).wait_recv()
            return carry

        lax.fori_loop(1, ns, landed, 0)

        def add(r, carry):
            band = pl.ds(pl.multiple_of(r * 16, 16), 16)
            total = rsbuf[g, 0, band, :].astype(F32)
            for j in range(1, ns):
                total += rsbuf[g, j, band, :].astype(F32)
            hg_all[g * ns + s, band, :] = total.astype(BF16)
            return carry

        lax.fori_loop(0, rows // 16, add, 0)

        def go(k, carry):
            ag_copy(g, k).start()
            return carry

        lax.fori_loop(1, ns, go, 0)

    def sb_copy(i):
        return remote(sb.at[i], sbs.at[i], sb_s.at[i], sb_r.at[i], dev(ec ^ 1, s))

    def activations(g):
        def landed(k, carry):
            slot = hg_all.at[g * ns + ((s - k) & (ns - 1))]
            remote(slot, slot, ag_s.at[g, k], ag_r.at[g, k], dev(ec, s)).wait_recv()
            return carry

        lax.fori_loop(1, ns, landed, 0)

        def act(p, carry):
            o = p // (rows // 16)
            band = pl.ds(pl.multiple_of((p % (rows // 16)) * 16, 16), 16)
            i = chunk_of(o)
            for h in range(2):
                lanes = pl.ds(h * hw, hw)
                grad = hg_all[o * 2 + h, band, :].astype(F32)
                gate = gu_all[i, h, 0, band, :].astype(F32)
                up = gu_all[i, h, 1, band, :].astype(F32)
                sig = jax.nn.sigmoid(gate)
                silu = gate * sig
                hid[o, band, lanes] = (silu * up).astype(BF16)
                gg[o, band, lanes] = (grad * up * sig * (1.0 + gate * (1.0 - sig))).astype(BF16)
                ug[o, band, lanes] = (grad * silu).astype(BF16)
            return carry

        n_bands = per_group * (rows // 16)
        lax.fori_loop(g * n_bands, (g + 1) * n_bands, act, 0)
        o0 = g * per_group
        shape = (per_group * rows, gg.shape[2])
        back = dot_nt(gg[pl.ds(o0, per_group)].reshape(shape), wg_ref[...]) + dot_nt(
            ug[pl.ds(o0, per_group)].reshape(shape), wu_ref[...]
        )
        back = back.astype(BF16)
        for r in range(per_group):
            i = chunk_of(o0 + r)
            sb[i] = back[r * rows : (r + 1) * rows]
            sb_copy(i).start()

    og_step(1)
    sib_copy(*og_sib, 0, 0, 1 - c).wait_recv()
    og_sib_wait(1)
    lax.fori_loop(0, 1, pick, 0)
    for k in range(1, side):
        for h in range(2):
            j = side - k
            gu_landed(gu_slot(h, j), h, 0, k)
            for k2 in range(1, side):
                gu_second(h, j, k2).start()
    tok_step(1, 0)

    def two_steps(m, carry):
        og_step(2 * m)
        tok_step(2 * m, 0)
        og_step(2 * m + 1)
        og_sib_wait(2 * m)
        og_sib_wait(2 * m + 1)
        tok_step(2 * m + 1, 0)
        lax.fori_loop(4 * m - 3, 4 * m + 1, pick, 0)
        partial_products(4 * m - 4, 4)
        return carry

    lax.fori_loop(1, quarter - 1, two_steps, 0)
    rs_start(0)
    two_steps(quarter - 1, 0)
    og_step(reach)
    og_sib_wait(reach)
    lax.fori_loop(n_chunks - 3, n_chunks, pick, 0)
    partial_products(n_chunks - 4, 4)
    rs_start(1)
    rs_finish(0)
    tok_step(reach, 0)
    tok_step(reach + 1, 0)
    rs_finish(1)
    lax.fori_loop(reach + 2, reach + 5, tok_step, 0)
    for k in range(1, side):
        for h in range(2):
            for j in range(side):
                m = side - k
                slot = seq_of(sy + m, sx + j) if h == 0 else seq_of(sy + j, sx + m)
                gu_landed(slot, h, 1 + j, k)
    activations(0)
    activations(1)
    lax.fori_loop(reach + 5, half_ring + 1, tok_step, 0)

    def contribution(chip):
        i = chip >> 1
        q = ((chip & 1) << 1) + c
        place = pos_ref[i]
        total = jnp.zeros((tok_rows, ig_ref.shape[1]), F32)
        for t, rowsrc in ((0, sb), (1, sbs)):
            mine = jnp.sum(jnp.where(row8 == t * 4 + q, place, 0.0), axis=0, keepdims=True)
            hot = (row80 == mine).astype(F32).astype(BF16)
            total += dot_tn(hot, rowsrc[i])
        return total

    def sb_landed(i, carry):
        sb_copy(i).wait_recv()
        return carry

    lax.fori_loop(0, n_chunks, sb_landed, 0)

    def target(way, chain, k):
        d = (reach if chain == 0 else half_ring) - k
        return at_z(d if way == 0 else nz - d), d

    def cb_copy(way, chain, k):
        chip, d = target(way, chain, k)
        hop = jnp.where((chain == 1) & (k == reach - 1), far, 1)
        nxt = at_z(jnp.where(way == 0, hop, nz - hop)) * 2 + c
        return remote(
            contrib.at[chip], rbuf.at[way, chain, k + 1], cb_s.at[way, chain, k],
            cb_r.at[way, chain, k + 1], dev(nxt, s),
        )

    def cb_landed(way, chain, k):
        slot = rbuf.at[way, chain, k]
        remote(slot, slot, cb_s.at[way, chain, 0], cb_r.at[way, chain, k], dev(ec, s)).wait_recv()

    chains = ((0, 0), (1, 0), (0, 1), (1, 1))

    def prepare(k):
        for way, chain in chains:
            chip, _ = target(way, chain, k)
            contrib[chip] = contribution(chip).astype(BF16)

    for way, chain in chains:
        if (way, chain) != (1, 1):
            chip, _ = target(way, chain, 0)
            contrib[chip] = contribution(chip).astype(BF16)
            cb_copy(way, chain, 0).start()

    def pick_tokens(o, carry):
        i = chunk_of(o)
        place = pos_ref[i]
        total = jnp.zeros((rows, tok_ref.shape[1]), F32)
        for q in range(4):
            hot = (row80 == place[q : q + 1, :]).astype(F32).astype(BF16)
            total += dot_nn(hot, tok_all[4 * i + q])
        xs[o] = total.astype(BF16)
        return carry

    def flat(ref):
        return ref[...].reshape(n_chunks * rows, ref.shape[2])

    def combine(k, carry):
        prepare(k)
        for way, chain in chains:

            def receive():
                chip, _ = target(way, chain, k)
                cb_landed(way, chain, k)
                contrib[chip] = (
                    contrib[chip].astype(F32) + rbuf[way, chain, k].astype(F32)
                ).astype(BF16)

            if (way, chain) == (1, 1):
                pl.when(k > 1)(receive)
            else:
                receive()
            cb_copy(way, chain, k).start()
        return carry

    combine(1, 0)
    sib_copy(*tk_sib, 0, 0, 1 - c).wait_recv()

    def tok_sib_wait(d, carry):
        sib_copy(*tk_sib, 0, d, 1 - c).wait_recv()

        @pl.when(d <= limit[1])
        def _():
            sib_copy(*tk_sib, 1, d, 1 - c).wait_recv()

        return carry

    lax.fori_loop(1, half_ring + 1, tok_sib_wait, 0)
    lax.fori_loop(0, n_chunks // 2, pick_tokens, 0)
    lax.fori_loop(2, min(3, reach), combine, 0)
    lax.fori_loop(n_chunks // 2, n_chunks, pick_tokens, 0)
    lax.fori_loop(min(3, reach), min(4, reach), combine, 0)
    gw_ref[...] = dot_tn(flat(xs), flat(gg)).astype(BF16)
    lax.fori_loop(min(4, reach), min(5, reach), combine, 0)
    uw_ref[...] = dot_tn(flat(xs), flat(ug)).astype(BF16)
    lax.fori_loop(min(5, reach), min(6, reach), combine, 0)
    dw_ref[...] = dot_tn(flat(gs), flat(hid)).T.astype(BF16)
    lax.fori_loop(min(6, reach), reach, combine, 0)
    final = contribution(z)
    for way, chain in chains:
        cb_landed(way, chain, reach)
        final += rbuf[way, chain, reach].astype(F32)
    ig_ref[...] = final.astype(BF16)

    def og_sent(k, carry):
        for way in (0, 1):

            @pl.when((k >= 1) & (k < reach))
            def _():
                ring_send(*og_x, way, k, k + 1).wait_send()

            @pl.when((k >= 1) & (reach + k < limit[way]))
            def _():
                ring_send(*og_x, way, reach + k, reach + k + 1).wait_send()

            @pl.when(k >= 1)
            def _():
                sib_copy(*og_sib, way, k, c).wait_send()

            @pl.when((k >= 1) & (reach + k <= limit[way]))
            def _():
                sib_copy(*og_sib, way, reach + k, c).wait_send()

        return carry

    def tok_sent(d, carry):
        for way in (0, 1):

            @pl.when(d < limit[way])
            def _():
                ring_send(*tk_x, way, d, d + 1).wait_send()

            @pl.when((d <= limit[way]) & ((d > 0) | (way == 0)))
            def _():
                sib_copy(*tk_sib, way, d, c).wait_send()

        return carry

    for way in (0, 1):
        ring_send(*og_x, way, 0, 1).wait_send()
        ring_send(*og_x, way, 0, far).wait_send()
    sib_copy(*og_sib, 0, 0, c).wait_send()
    lax.fori_loop(1, reach + 1, og_sent, 0)
    lax.fori_loop(0, half_ring + 1, tok_sent, 0)
    for k in range(1, side):
        for h in range(2):
            gu_first(h, k).wait_send()
            for j in range(side):
                gu_second(h, j, k).wait_send()

    def seq_sent(k, carry):
        for g in range(2):
            rs_copy(g, k).wait_send()
            ag_copy(g, k).wait_send()
        return carry

    lax.fori_loop(1, ns, seq_sent, 0)

    def sb_sent(i, carry):
        sb_copy(i).wait_send()
        return carry

    lax.fori_loop(0, n_chunks, sb_sent, 0)

    def cb_sent(k, carry):
        for way, chain in chains:
            if (way, chain) == (1, 1):

                @pl.when(k > 0)
                def _():
                    cb_copy(way, chain, k).wait_send()
            else:
                cb_copy(way, chain, k).wait_send()
        return carry

    lax.fori_loop(0, reach, cb_sent, 0)


def per_device(
    tokens, out_grad, expert_ids, router_probs, keep_mask, gate_saved, up_saved, w_gate, w_up, w_down
):
    nz = lax.axis_size("expert") // 2
    ns = lax.axis_size("seq")
    side = {4: 2, 16: 4}[ns]
    tok_rows, width = tokens.shape
    rows, ff = gate_saved.shape[1:]
    cap = rows // 4
    n_chunks = nz // 2
    hw = ff // 2
    reach = nz // 4
    dma = pltpu.SemaphoreType.DMA
    vmem = pl.BlockSpec(memory_space=pltpu.VMEM)
    ring = (2, nz // 2 + 1)
    out = pl.pallas_call(
        functools.partial(layer_kernel, nz, side, cap),
        out_shape=(
            jax.ShapeDtypeStruct((tok_rows, width), BF16),
            jax.ShapeDtypeStruct((width, ff), BF16),
            jax.ShapeDtypeStruct((width, ff), BF16),
            jax.ShapeDtypeStruct((ff, width), BF16),
        ),
        in_specs=[vmem] * 10,
        out_specs=(vmem,) * 4,
        scratch_shapes=[
            pltpu.VMEM((2 * nz, tok_rows + 16, width), BF16),
            pltpu.VMEM((2 * nz, tok_rows, width), BF16),
            pltpu.VMEM((ns, 2, 2, rows, hw), BF16),
            pltpu.VMEM((2 * ns, rows, hw), BF16),
            pltpu.VMEM((2, ns, rows, hw), BF16),
            pltpu.VMEM((2 * ns, rows, hw), BF16),
            pltpu.VMEM((n_chunks, rows, ff), BF16),
            pltpu.VMEM((n_chunks, rows, ff), BF16),
            pltpu.VMEM((n_chunks, rows, ff), BF16),
            pltpu.VMEM((n_chunks, rows, width), BF16),
            pltpu.VMEM((n_chunks, rows, width), BF16),
            pltpu.VMEM((n_chunks, rows, width), BF16),
            pltpu.VMEM((n_chunks, rows, width), BF16),
            pltpu.VMEM((n_chunks, 8, tok_rows), F32),
            pltpu.VMEM((nz, tok_rows, width), BF16),
            pltpu.VMEM((2, 2, reach + 1, tok_rows, width), BF16),
            dma(ring), dma(ring), dma(ring), dma(ring),
            dma(ring), dma(ring), dma(ring), dma(ring),
            dma((2, side + 1, side)), dma((2, side + 1, side)),
            dma((2, ns)), dma((2, ns)), dma((2, ns)), dma((2, ns)),
            dma((n_chunks,)), dma((n_chunks,)),
            dma((2, 2, reach + 1)), dma((2, 2, reach + 1)),
        ],
        compiler_params=pltpu.CompilerParams(
            collective_id=0, has_side_effects=True, vmem_limit_bytes=56 << 20
        ),
        cost_estimate=pl.CostEstimate(flops=3 << 30, bytes_accessed=4 << 20, transcendentals=1 << 20),
    )(
        tokens, out_grad, expert_ids.T, router_probs.T, keep_mask.T, gate_saved[0], up_saved[0],
        w_gate[0], w_up[0], w_down[0],
    )
    return (out[0], out[1][None], out[2][None], out[3][None])


def solution(mesh):
    return jax.shard_map(
        per_device,
        mesh=mesh,
        in_specs=(
            P("expert", "seq"),
            P("expert", "seq"),
            P("expert", None),
            P("expert", None),
            P("expert", None),
            P("expert", "seq", None),
            P("expert", "seq", None),
            P("expert", "seq", None),
            P("expert", "seq", None),
            P("expert", None, "seq"),
        ),
        out_specs=(
            P("expert", "seq"),
            P("expert", "seq", None),
            P("expert", "seq", None),
            P("expert", None, "seq"),
        ),
        check_vma=False,
    )
```

```python
import functools

import jax
import jax.numpy as jnp
from jax import lax
from jax.experimental import pallas as pl
from jax.experimental.pallas import tpu as pltpu
from jax.sharding import PartitionSpec as P

MESH = pl.DeviceIdType.MESH
F32 = jnp.float32
BF16 = jnp.bfloat16


def dot_nt(a, b):
    return lax.dot_general(a, b, (((1,), (1,)), ((), ())), preferred_element_type=F32)


def dot_tn(a, b):
    return lax.dot_general(a, b, (((0,), (0,)), ((), ())), preferred_element_type=F32)


def dot_nn(a, b):
    return lax.dot_general(a, b, (((1,), (0,)), ((), ())), preferred_element_type=F32)


def layer_kernel(
    nz, side, cap,
    tok_ref, og_ref, ids_in, prob_in, keep_in, gate_ref, up_ref, wg_in, wu_in, wd_in,
    ig_ref, gw_ref, uw_ref, dw_ref,
    og_all, tok_all, gu_all, pbuf, rsbuf, hg_all, gg, ug, hid, gs, xs, sb, sbs, pos_ref, contrib, rbuf,
    og_s, og_r, og_ss, og_sr, tk_s, tk_r, tk_ss, tk_sr, gu_s, gu_r, rs_s, rs_r, ag_s, ag_r, sb_s, sb_r,
    cb_s, cb_r, ids_ref, prob_ref, keep_ref, wg_ref, wu_ref, wd_ref, load_s,
):
    ns = side * side
    ec = lax.axis_index("expert")
    s = lax.axis_index("seq")
    z, c = ec >> 1, ec & 1
    sy, sx = s // side, s % side
    half_ring = nz // 2
    reach = half_ring // 2
    far = reach + 1
    limit = (half_ring, half_ring - 1)
    n_chunks = nz // 2
    quarter = reach // 2
    tok_rows = og_ref.shape[0]
    rows = 4 * cap
    hw = gate_ref.shape[1] // 2
    per_group = n_chunks // 2

    def at_z(k):
        return (z + k) & (nz - 1)

    def dev(e, q):
        return {"expert": e, "seq": q}

    def remote(src, dst, ssem, rsem, device):
        return pltpu.make_async_remote_copy(
            src, dst, ssem, rsem, device_id=device, device_id_type=MESH
        )

    small = [(ids_in, ids_ref), (prob_in, prob_ref), (keep_in, keep_ref)]
    small += [(og_ref, og_all.at[ec, pl.ds(0, tok_rows)]), (tok_ref, tok_all.at[ec])]
    saved = [
        (ref.at[:, pl.ds(h * hw, hw)], gu_all.at[s, h, a])
        for h in range(2)
        for a, ref in ((0, gate_ref), (1, up_ref))
    ]
    large = [(wd_in, wd_ref), (wg_in, wg_ref), (wu_in, wu_ref)]
    loads = [
        pltpu.make_async_copy(src, dst, load_s.at[n])
        for n, (src, dst) in enumerate(small + saved + large)
    ]
    for load in loads:
        load.start()

    bar = pltpu.get_barrier_semaphore()
    hops = sorted({1, nz - 1, far, nz - far})
    for k in hops:
        pl.semaphore_signal(bar, inc=1, device_id=dev(at_z(k) * 2 + c, s), device_id_type=MESH)
    pl.semaphore_signal(bar, inc=1, device_id=dev(ec ^ 1, s), device_id_type=MESH)

    def greet(k, carry):
        pl.semaphore_signal(bar, inc=1, device_id=dev(ec, (s + k) & (ns - 1)), device_id_type=MESH)
        return carry

    lax.fori_loop(1, ns, greet, 0)

    for load in loads[:5]:
        load.wait()
    weight = prob_ref[...] * keep_ref[...].astype(F32)
    w_hi = weight.astype(BF16).astype(F32)
    w_mid = (weight - w_hi).astype(BF16).astype(F32)
    w_lo = (weight - w_hi) - w_mid
    top = jnp.concatenate([ids_ref[...].astype(F32), w_mid], axis=1)
    low = jnp.concatenate([w_hi, w_lo], axis=1)
    og_all[ec, pl.ds(tok_rows, 16), :] = jnp.concatenate([top, low], axis=0).astype(BF16)
    pl.semaphore_wait(bar, len(hops) + 1 + ns - 1)

    def zslot(way, d, core):
        return at_z(nz - d if way == 0 else d) * 2 + core

    def ring_send(buf, ssem, rsem, way, d, child):
        k = child - d
        slot = zslot(way, d, c)
        target = at_z(k if way == 0 else nz - k) * 2 + c
        return remote(
            buf.at[slot], buf.at[slot], ssem.at[way, child], rsem.at[way, child], dev(target, s)
        )

    def ring_landed(buf, ssem, rsem, way, d):
        slot = buf.at[zslot(way, d, c)]
        remote(slot, slot, ssem.at[way, d], rsem.at[way, d], dev(ec, s)).wait_recv()

    def sib_copy(buf, ssem, rsem, way, d, core):
        slot = buf.at[zslot(way, d, core)]
        return remote(slot, slot, ssem.at[way, d], rsem.at[way, d], dev(ec ^ 1, s))

    og_x = (og_all, og_s, og_r)
    og_sib = (og_all, og_ss, og_sr)
    tk_x = (tok_all, tk_s, tk_r)
    tk_sib = (tok_all, tk_ss, tk_sr)

    for way in (0, 1):
        ring_send(*og_x, way, 0, 1).start()
        ring_send(*og_x, way, 0, far).start()
    sib_copy(*og_sib, 0, 0, c).start()

    def seq_of(y, x):
        return (y & (side - 1)) * side + (x & (side - 1))

    def gu_peer(h, phase, k):
        return seq_of(sy, sx + k) if (h == phase) else seq_of(sy + k, sx)

    def gu_slot(h, j):
        return seq_of(sy, sx + j) if h == 0 else seq_of(sy + j, sx)

    def gu_first(h, k):
        return remote(
            gu_all.at[s, h], gu_all.at[s, h], gu_s.at[h, 0, k], gu_r.at[h, 0, k],
            dev(ec, gu_peer(h, 0, k)),
        )

    def gu_second(h, j, k):
        slot = gu_all.at[gu_slot(h, j), h]
        return remote(
            slot, slot, gu_s.at[h, 1 + j, k], gu_r.at[h, 1 + j, k], dev(ec, gu_peer(h, 1, k))
        )

    def gu_landed(slot, h, a, k):
        ref = gu_all.at[slot, h]
        remote(ref, ref, gu_s.at[h, a, k], gu_r.at[h, a, k], dev(ec, s)).wait_recv()

    for load in loads[5:9]:
        load.wait()
    for k in range(1, side):
        for h in range(2):
            gu_first(h, k).start()
    for k in range(1, side):
        for h in range(2):
            gu_second(h, 0, k).start()
    for way in (0, 1):
        ring_send(*tk_x, way, 0, 1).start()
    sib_copy(*tk_sib, 0, 0, c).start()

    def og_step(k):
        for way in (0, 1):
            ring_landed(*og_x, way, k)

            @pl.when(k < reach)
            def _():
                ring_send(*og_x, way, k, k + 1).start()

            sib_copy(*og_sib, way, k, c).start()

            def far_part():
                ring_landed(*og_x, way, reach + k)

                @pl.when(reach + k < limit[way])
                def _():
                    ring_send(*og_x, way, reach + k, reach + k + 1).start()

                sib_copy(*og_sib, way, reach + k, c).start()

            if way == 0:
                far_part()
            else:
                pl.when(reach + k <= limit[1])(far_part)

    def og_sib_wait(k):
        for way in (0, 1):
            sib_copy(*og_sib, way, k, 1 - c).wait_recv()
            if way == 0:
                sib_copy(*og_sib, way, reach + k, 1 - c).wait_recv()
            else:

                @pl.when(reach + k <= limit[1])
                def _():
                    sib_copy(*og_sib, way, reach + k, 1 - c).wait_recv()

    def tok_step(d, carry):
        for way in (0, 1):

            def part():
                ring_landed(*tk_x, way, d)

                @pl.when(d < limit[way])
                def _():
                    ring_send(*tk_x, way, d, d + 1).start()

                sib_copy(*tk_sib, way, d, c).start()

            if way == 0:
                part()
            else:
                pl.when(d <= limit[1])(part)
        return carry

    row80 = lax.broadcasted_iota(jnp.int32, (rows, tok_rows), 0).astype(F32)
    row8 = lax.broadcasted_iota(jnp.int32, (8, tok_rows), 0)
    before = (
        lax.broadcasted_iota(jnp.int32, (tok_rows, tok_rows), 0)
        < lax.broadcasted_iota(jnp.int32, (tok_rows, tok_rows), 1)
    ).astype(F32).astype(BF16)

    def chunk_at(offset):
        return ((z >> 1) + offset) & (n_chunks - 1)

    def chunk_of(o):
        m = ((o - 1) >> 2) + 1
        r = (o - 1) & 3
        last = o - (n_chunks - 3)
        plain = (m + jnp.where(r >= 2, quarter, 0)) * jnp.where((r & 1) == 1, -1, 1)
        tail = jnp.where(last == 0, quarter, jnp.where(last == 1, -quarter, n_chunks // 2))
        off = jnp.where(o == 0, 0, jnp.where(last >= 0, tail, plain))
        return chunk_at(off + n_chunks)

    def pick(o, carry):
        i = chunk_of(o)
        member = jnp.zeros((8, tok_rows), F32)
        ws = []
        for q in range(4):
            meta = og_all[4 * i + q, pl.ds(tok_rows, 16), :].astype(F32)
            ids = meta[0:8, 0:tok_rows]
            w = (meta[8:16, 0:tok_rows] + meta[0:8, tok_rows:]) + meta[8:16, tok_rows:]
            for t in range(2):
                own = (ids == (ec if t == 0 else ec ^ 1).astype(F32)).astype(F32)
                member = jnp.where(
                    row8 == t * 4 + q, jnp.sum(own, axis=0, keepdims=True), member
                )
                if t == 0:
                    ws.append(jnp.sum(own * w, axis=0, keepdims=True))
        count = dot_nn(member.astype(BF16), before)
        place = jnp.where(member > 0.5, count + ((row8 & 3) * cap).astype(F32), -1000.0)
        pos_ref[i] = place
        total = jnp.zeros((rows, og_ref.shape[1]), F32)
        wsum = jnp.zeros((rows, 1), F32)
        for q in range(4):
            hot = (row80 == place[q : q + 1, :]).astype(F32)
            total += dot_nn(hot.astype(BF16), og_all[4 * i + q, pl.ds(0, tok_rows), :])
            wsum += jnp.sum(hot * ws[q], axis=1, keepdims=True)
        gs[o] = (total * wsum).astype(BF16)
        return carry

    def partial_products(m, count):
        left = gs[pl.ds(m, count)].reshape(count * rows, gs.shape[2])
        out = dot_nt(left, wd_ref[...]).astype(BF16)
        for r in range(count):
            o = m + r
            for h in range(2):
                pbuf[o * 2 + h] = out[r * rows : (r + 1) * rows, h * hw : (h + 1) * hw]

    def rs_copy(g, k):
        j = (s + k) & (ns - 1)
        return remote(
            pbuf.at[g * ns + j], rsbuf.at[g, s], rs_s.at[g, k], rs_r.at[g, k], dev(ec, j)
        )

    def rs_start(g):
        def go(k, carry):
            rs_copy(g, k).start()
            return carry

        lax.fori_loop(1, ns, go, 0)
        rsbuf[g, s] = pbuf[g * ns + s]

    def ag_copy(g, k):
        piece = hg_all.at[g * ns + s]
        return remote(piece, piece, ag_s.at[g, k], ag_r.at[g, k], dev(ec, (s + k) & (ns - 1)))

    def rs_finish(g):
        def landed(k, carry):
            slot = rsbuf.at[g, (s - k) & (ns - 1)]
            remote(slot, slot, rs_s.at[g, k], rs_r.at[g, k], dev(ec, s)).wait_recv()
            return carry

        lax.fori_loop(1, ns, landed, 0)

        def add(r, carry):
            band = pl.ds(pl.multiple_of(r * 16, 16), 16)
            total = rsbuf[g, 0, band, :].astype(F32)
            for j in range(1, ns):
                total += rsbuf[g, j, band, :].astype(F32)
            hg_all[g * ns + s, band, :] = total.astype(BF16)
            return carry

        lax.fori_loop(0, rows // 16, add, 0)

        def go(k, carry):
            ag_copy(g, k).start()
            return carry

        lax.fori_loop(1, ns, go, 0)

    def sb_copy(i):
        return remote(sb.at[i], sbs.at[i], sb_s.at[i], sb_r.at[i], dev(ec ^ 1, s))

    def activations(g):
        def landed(k, carry):
            slot = hg_all.at[g * ns + ((s - k) & (ns - 1))]
            remote(slot, slot, ag_s.at[g, k], ag_r.at[g, k], dev(ec, s)).wait_recv()
            return carry

        lax.fori_loop(1, ns, landed, 0)

        def act(p, carry):
            o = p // (rows // 16)
            band = pl.ds(pl.multiple_of((p % (rows // 16)) * 16, 16), 16)
            i = chunk_of(o)
            for h in range(2):
                lanes = pl.ds(h * hw, hw)
                grad = hg_all[o * 2 + h, band, :].astype(F32)
                gate = gu_all[i, h, 0, band, :].astype(F32)
                up = gu_all[i, h, 1, band, :].astype(F32)
                sig = jax.nn.sigmoid(gate)
                silu = gate * sig
                hid[o, band, lanes] = (silu * up).astype(BF16)
                gg[o, band, lanes] = (grad * up * sig * (1.0 + gate * (1.0 - sig))).astype(BF16)
                ug[o, band, lanes] = (grad * silu).astype(BF16)
            return carry

        n_bands = per_group * (rows // 16)
        lax.fori_loop(g * n_bands, (g + 1) * n_bands, act, 0)
        o0 = g * per_group
        shape = (per_group * rows, gg.shape[2])
        back = dot_nt(gg[pl.ds(o0, per_group)].reshape(shape), wg_ref[...]) + dot_nt(
            ug[pl.ds(o0, per_group)].reshape(shape), wu_ref[...]
        )
        back = back.astype(BF16)
        for r in range(per_group):
            i = chunk_of(o0 + r)
            sb[i] = back[r * rows : (r + 1) * rows]
            sb_copy(i).start()

    og_step(1)
    sib_copy(*og_sib, 0, 0, 1 - c).wait_recv()
    og_sib_wait(1)
    lax.fori_loop(0, 1, pick, 0)
    for k in range(1, side):
        for h in range(2):
            j = side - k
            gu_landed(gu_slot(h, j), h, 0, k)
            for k2 in range(1, side):
                gu_second(h, j, k2).start()
    tok_step(1, 0)

    def two_steps(m, carry):
        og_step(2 * m)
        tok_step(2 * m, 0)
        og_step(2 * m + 1)
        og_sib_wait(2 * m)
        og_sib_wait(2 * m + 1)
        tok_step(2 * m + 1, 0)
        lax.fori_loop(4 * m - 3, 4 * m + 1, pick, 0)
        partial_products(4 * m - 4, 4)
        return carry

    loads[9].wait()
    lax.fori_loop(1, quarter - 1, two_steps, 0)
    rs_start(0)
    two_steps(quarter - 1, 0)
    og_step(reach)
    og_sib_wait(reach)
    lax.fori_loop(n_chunks - 3, n_chunks, pick, 0)
    partial_products(n_chunks - 4, 4)
    rs_start(1)
    rs_finish(0)
    tok_step(reach, 0)
    tok_step(reach + 1, 0)
    rs_finish(1)
    lax.fori_loop(reach + 2, reach + 5, tok_step, 0)
    for k in range(1, side):
        for h in range(2):
            for j in range(side):
                m = side - k
                slot = seq_of(sy + m, sx + j) if h == 0 else seq_of(sy + j, sx + m)
                gu_landed(slot, h, 1 + j, k)
    loads[10].wait()
    loads[11].wait()
    activations(0)
    activations(1)
    lax.fori_loop(reach + 5, half_ring + 1, tok_step, 0)

    def contribution(chip):
        i = chip >> 1
        q = ((chip & 1) << 1) + c
        place = pos_ref[i]
        total = jnp.zeros((tok_rows, ig_ref.shape[1]), F32)
        for t, rowsrc in ((0, sb), (1, sbs)):
            mine = jnp.sum(jnp.where(row8 == t * 4 + q, place, 0.0), axis=0, keepdims=True)
            hot = (row80 == mine).astype(F32).astype(BF16)
            total += dot_tn(hot, rowsrc[i])
        return total

    def sb_landed(i, carry):
        sb_copy(i).wait_recv()
        return carry

    lax.fori_loop(0, n_chunks, sb_landed, 0)

    def target(way, chain, k):
        d = (reach if chain == 0 else half_ring) - k
        return at_z(d if way == 0 else nz - d), d

    def cb_copy(way, chain, k):
        chip, d = target(way, chain, k)
        hop = jnp.where((chain == 1) & (k == reach - 1), far, 1)
        nxt = at_z(jnp.where(way == 0, hop, nz - hop)) * 2 + c
        return remote(
            contrib.at[chip], rbuf.at[way, chain, k + 1], cb_s.at[way, chain, k],
            cb_r.at[way, chain, k + 1], dev(nxt, s),
        )

    def cb_landed(way, chain, k):
        slot = rbuf.at[way, chain, k]
        remote(slot, slot, cb_s.at[way, chain, 0], cb_r.at[way, chain, k], dev(ec, s)).wait_recv()

    chains = ((0, 0), (1, 0), (0, 1), (1, 1))

    def prepare(k):
        for way, chain in chains:
            chip, _ = target(way, chain, k)
            contrib[chip] = contribution(chip).astype(BF16)

    for way, chain in chains:
        if (way, chain) != (1, 1):
            chip, _ = target(way, chain, 0)
            contrib[chip] = contribution(chip).astype(BF16)
            cb_copy(way, chain, 0).start()

    def pick_tokens(o, carry):
        i = chunk_of(o)
        place = pos_ref[i]
        total = jnp.zeros((rows, tok_ref.shape[1]), F32)
        for q in range(4):
            hot = (row80 == place[q : q + 1, :]).astype(F32).astype(BF16)
            total += dot_nn(hot, tok_all[4 * i + q])
        xs[o] = total.astype(BF16)
        return carry

    def flat(ref):
        return ref[...].reshape(n_chunks * rows, ref.shape[2])

    def combine(k, carry):
        prepare(k)
        for way, chain in chains:

            def receive():
                chip, _ = target(way, chain, k)
                cb_landed(way, chain, k)
                contrib[chip] = (
                    contrib[chip].astype(F32) + rbuf[way, chain, k].astype(F32)
                ).astype(BF16)

            if (way, chain) == (1, 1):
                pl.when(k > 1)(receive)
            else:
                receive()
            cb_copy(way, chain, k).start()
        return carry

    combine(1, 0)
    sib_copy(*tk_sib, 0, 0, 1 - c).wait_recv()

    def tok_sib_wait(d, carry):
        sib_copy(*tk_sib, 0, d, 1 - c).wait_recv()

        @pl.when(d <= limit[1])
        def _():
            sib_copy(*tk_sib, 1, d, 1 - c).wait_recv()

        return carry

    lax.fori_loop(1, half_ring + 1, tok_sib_wait, 0)
    lax.fori_loop(0, n_chunks // 2, pick_tokens, 0)
    lax.fori_loop(2, min(3, reach), combine, 0)
    lax.fori_loop(n_chunks // 2, n_chunks, pick_tokens, 0)
    lax.fori_loop(min(3, reach), min(4, reach), combine, 0)
    gw_ref[...] = dot_tn(flat(xs), flat(gg)).astype(BF16)
    lax.fori_loop(min(4, reach), min(5, reach), combine, 0)
    uw_ref[...] = dot_tn(flat(xs), flat(ug)).astype(BF16)
    lax.fori_loop(min(5, reach), min(6, reach), combine, 0)
    dw_ref[...] = dot_tn(flat(gs), flat(hid)).T.astype(BF16)
    lax.fori_loop(min(6, reach), reach, combine, 0)
    final = contribution(z)
    for way, chain in chains:
        cb_landed(way, chain, reach)
        final += rbuf[way, chain, reach].astype(F32)
    ig_ref[...] = final.astype(BF16)

    def og_sent(k, carry):
        for way in (0, 1):

            @pl.when((k >= 1) & (k < reach))
            def _():
                ring_send(*og_x, way, k, k + 1).wait_send()

            @pl.when((k >= 1) & (reach + k < limit[way]))
            def _():
                ring_send(*og_x, way, reach + k, reach + k + 1).wait_send()

            @pl.when(k >= 1)
            def _():
                sib_copy(*og_sib, way, k, c).wait_send()

            @pl.when((k >= 1) & (reach + k <= limit[way]))
            def _():
                sib_copy(*og_sib, way, reach + k, c).wait_send()

        return carry

    def tok_sent(d, carry):
        for way in (0, 1):

            @pl.when(d < limit[way])
            def _():
                ring_send(*tk_x, way, d, d + 1).wait_send()

            @pl.when((d <= limit[way]) & ((d > 0) | (way == 0)))
            def _():
                sib_copy(*tk_sib, way, d, c).wait_send()

        return carry

    for way in (0, 1):
        ring_send(*og_x, way, 0, 1).wait_send()
        ring_send(*og_x, way, 0, far).wait_send()
    sib_copy(*og_sib, 0, 0, c).wait_send()
    lax.fori_loop(1, reach + 1, og_sent, 0)
    lax.fori_loop(0, half_ring + 1, tok_sent, 0)
    for k in range(1, side):
        for h in range(2):
            gu_first(h, k).wait_send()
            for j in range(side):
                gu_second(h, j, k).wait_send()

    def seq_sent(k, carry):
        for g in range(2):
            rs_copy(g, k).wait_send()
            ag_copy(g, k).wait_send()
        return carry

    lax.fori_loop(1, ns, seq_sent, 0)

    def sb_sent(i, carry):
        sb_copy(i).wait_send()
        return carry

    lax.fori_loop(0, n_chunks, sb_sent, 0)

    def cb_sent(k, carry):
        for way, chain in chains:
            if (way, chain) == (1, 1):

                @pl.when(k > 0)
                def _():
                    cb_copy(way, chain, k).wait_send()
            else:
                cb_copy(way, chain, k).wait_send()
        return carry

    lax.fori_loop(0, reach, cb_sent, 0)


def per_device(
    tokens, out_grad, expert_ids, router_probs, keep_mask, gate_saved, up_saved, w_gate, w_up, w_down
):
    nz = lax.axis_size("expert") // 2
    ns = lax.axis_size("seq")
    side = {4: 2, 16: 4}[ns]
    tok_rows, width = tokens.shape
    rows, ff = gate_saved.shape[1:]
    cap = rows // 4
    n_chunks = nz // 2
    hw = ff // 2
    reach = nz // 4
    dma = pltpu.SemaphoreType.DMA
    vmem = pl.BlockSpec(memory_space=pltpu.VMEM)
    ring = (2, nz // 2 + 1)
    out = pl.pallas_call(
        functools.partial(layer_kernel, nz, side, cap),
        out_shape=(
            jax.ShapeDtypeStruct((tok_rows, width), BF16),
            jax.ShapeDtypeStruct((width, ff), BF16),
            jax.ShapeDtypeStruct((width, ff), BF16),
            jax.ShapeDtypeStruct((ff, width), BF16),
        ),
        in_specs=[pl.BlockSpec(memory_space=pltpu.HBM)] * 10,
        out_specs=(vmem,) * 4,
        scratch_shapes=[
            pltpu.VMEM((2 * nz, tok_rows + 16, width), BF16),
            pltpu.VMEM((2 * nz, tok_rows, width), BF16),
            pltpu.VMEM((ns, 2, 2, rows, hw), BF16),
            pltpu.VMEM((2 * ns, rows, hw), BF16),
            pltpu.VMEM((2, ns, rows, hw), BF16),
            pltpu.VMEM((2 * ns, rows, hw), BF16),
            pltpu.VMEM((n_chunks, rows, ff), BF16),
            pltpu.VMEM((n_chunks, rows, ff), BF16),
            pltpu.VMEM((n_chunks, rows, ff), BF16),
            pltpu.VMEM((n_chunks, rows, width), BF16),
            pltpu.VMEM((n_chunks, rows, width), BF16),
            pltpu.VMEM((n_chunks, rows, width), BF16),
            pltpu.VMEM((n_chunks, rows, width), BF16),
            pltpu.VMEM((n_chunks, 8, tok_rows), F32),
            pltpu.VMEM((nz, tok_rows, width), BF16),
            pltpu.VMEM((2, 2, reach + 1, tok_rows, width), BF16),
            dma(ring), dma(ring), dma(ring), dma(ring),
            dma(ring), dma(ring), dma(ring), dma(ring),
            dma((2, side + 1, side)), dma((2, side + 1, side)),
            dma((2, ns)), dma((2, ns)), dma((2, ns)), dma((2, ns)),
            dma((n_chunks,)), dma((n_chunks,)),
            dma((2, 2, reach + 1)), dma((2, 2, reach + 1)),
            pltpu.VMEM(expert_ids.shape[::-1], jnp.int32),
            pltpu.VMEM(router_probs.shape[::-1], F32),
            pltpu.VMEM(keep_mask.shape[::-1], jnp.int32),
            pltpu.VMEM((width, ff), BF16), pltpu.VMEM((width, ff), BF16),
            pltpu.VMEM((ff, width), BF16),
            dma((12,)),
        ],
        compiler_params=pltpu.CompilerParams(
            collective_id=0, has_side_effects=True, vmem_limit_bytes=56 << 20
        ),
        cost_estimate=pl.CostEstimate(flops=3 << 30, bytes_accessed=4 << 20, transcendentals=1 << 20),
    )(
        tokens, out_grad, expert_ids.T, router_probs.T, keep_mask.T, gate_saved[0], up_saved[0],
        w_gate[0], w_up[0], w_down[0],
    )
    return (out[0], out[1][None], out[2][None], out[3][None])


def solution(mesh):
    return jax.shard_map(
        per_device,
        mesh=mesh,
        in_specs=(
            P("expert", "seq"),
            P("expert", "seq"),
            P("expert", None),
            P("expert", None),
            P("expert", None),
            P("expert", "seq", None),
            P("expert", "seq", None),
            P("expert", "seq", None),
            P("expert", "seq", None),
            P("expert", None, "seq"),
        ),
        out_specs=(
            P("expert", "seq"),
            P("expert", "seq", None),
            P("expert", "seq", None),
            P("expert", None, "seq"),
        ),
        check_vma=False,
    )
```
